32 devices in a mesh: grp: 2 (over y), tok: 4 (over x, core), mdl: 4 (over z).
Axes of the slice: x: 2, y: 2, z: 4, core: 2. Of those that a mesh axis runs over, the one named last changes fastest.
Arguments:
- tokens: bfloat16 [1024, 8192], P(('grp', 'tok'), 'mdl'), parts along dimension 0, may hold values from -6 to 6
- in_weight: bfloat16 [4096, 3, 8192], P('tok', None, 'mdl'), may hold values from -0.0625 to 0.0625
- short_weight: float32 [4096, 3, 3], P(('tok', 'mdl')), may hold values from -3 to 3
- long_filter: float32 [256, 128], P(('tok', 'mdl')), may hold values from -0.6 to 0.6
- skip_bias: float32 [4096], P(('tok', 'mdl')), may hold values from 0.5 to 1.5
Outputs:
- mixed: bfloat16 [4096, 1024], P('tok', ('grp', 'mdl')), parts along dimension 1
The draws below stay inside these ranges and needn't reach their ends.
There are 2 independent parts, one for each index of `grp`. The reference program is written for one: setup_inputs(seed, part) draws one part's arguments, and reference() takes and returns one part's arrays. A program takes and returns all parts, laid end to end along the dimension named above; an argument that names none is the same for every part. Nothing has to cross between parts.
All inputs are finite; a program needn't handle non-finite values.
Results may differ from the reference program's by a relative error of at most 0.017.
Values may be sent and summed in bfloat16 or wider, within the bound.
A program may use at most 128 MiB of HBM per device.

```python
import math
import jax
import jax.numpy as jnp
from jax import lax

D = 8192
H = 4096
GROUP = 16
TAPS = 128
TOKENS = 512
DBLOCK = 2048


def draw_long_filter(key, part):
    key = jax.random.fold_in(key, 7)
    key_rate, key_taps = jax.random.split(key)
    filter_count = H // GROUP
    decay_rates = jnp.exp(jax.random.uniform(key_rate, (filter_count, 1), jnp.float32, math.log(0.0005), math.log(0.08)))
    random_taps = jnp.clip(jax.random.normal(key_taps, (filter_count, TAPS), jnp.float32), -4.0, 4.0)
    tap_index = jnp.arange(TAPS, dtype=jnp.float32)[None, :]
    return 0.15 * random_taps * jnp.exp(-decay_rates * tap_index)


def levels(key, dims, pieces, smallest, high):
    level = 1.0
    for position, blocks in pieces:
        heights = jax.random.uniform(jax.random.fold_in(jax.random.fold_in(key, 6), position), (blocks,), jnp.float32, smallest / len(pieces), high / len(pieces))
        level = level * jnp.repeat(jnp.exp(heights), dims[position] // blocks).reshape((-1,) + (1,) * (len(dims) - 1 - position))
    return level


def gaussian(own_key, extent, deviation, most, shards=(), kind=jnp.bfloat16):
    values = jax.random.normal(own_key, extent, jnp.float32) * deviation
    if len(shards) > 0:
        values = levels(own_key, extent, shards, -0.22, 0.18) * values
    return jnp.clip(values, min=-most, max=most).astype(kind)


def setup_inputs(seed: int = 0, part: int = 0) -> dict:
    key_list = jax.random.split(jax.random.key(seed), 6)
    own_keys = jax.random.split(jax.random.fold_in(key_list[5], part), 6)
    tokens = gaussian(own_keys[0], (TOKENS, D), 1.0, 6.0, ((0, 4), (1, 4)))
    in_weight = gaussian(key_list[1], (H, 3, D), D ** -0.5, 0.0625, ((0, 4), (2, 4)))
    short_weight = gaussian(key_list[2], (H, 3, 3), 0.6, 3.0, ((0, 16),), jnp.float32)
    long_filter = draw_long_filter(jax.random.fold_in(key_list[5], 71), part)
    skip_bias = jnp.clip(0.5 + 1.0 * jax.random.uniform(key_list[4], (H,), jnp.float32) ** levels(key_list[4], (H,), ((0, 16),), -0.2, 0.2), 0.5, 1.5)
    return {"tokens": tokens, "in_weight": in_weight, "short_weight": short_weight, "long_filter": long_filter, "skip_bias": skip_bias}


def project(tokens, in_weight):
    block_count = D // DBLOCK
    flat_weight = in_weight.reshape(H * 3, D)

    def add_block(running, block_index):
        begin_at = (block_index * DBLOCK).astype(jnp.int32)
        block_rows = lax.dynamic_slice_in_dim(tokens, begin_at, DBLOCK, 1)
        block_weight = lax.dynamic_slice_in_dim(flat_weight, begin_at, DBLOCK, 1)
        partial_term = lax.dot_general(block_rows, block_weight, (((1,), (1,)), ((), ())), preferred_element_type=jnp.float32)
        rounded = lax.optimization_barrier(partial_term.astype(jnp.bfloat16))
        return running + rounded.astype(jnp.float32), None

    running, _ = lax.scan(add_block, jnp.zeros((TOKENS, H * 3), jnp.float32), jnp.arange(block_count, dtype=jnp.int32))
    return running.reshape(TOKENS, H, 3)


def reference(tokens, in_weight, short_weight, long_filter, skip_bias):
    projected = project(tokens, in_weight)
    padded = jnp.pad(projected, ((2, 0), (0, 0), (0, 0)))
    featured = jnp.zeros((TOKENS, H, 3), jnp.float32)
    for shift_index in range(3):
        featured = featured + short_weight[None, :, :, shift_index] * padded[2 - shift_index:2 - shift_index + TOKENS]
    queries = featured[:, :, 0]
    product = featured[:, :, 1] * featured[:, :, 2]
    channel_taps = jnp.repeat(long_filter, GROUP, axis=0).T

    def apply_tap(state_pair, tap_number):
        accumulated, shifted = state_pair
        accumulated = accumulated + shifted * channel_taps[tap_number][None, :]
        shifted = jnp.concatenate([jnp.zeros((1, H), jnp.float32), shifted[:-1]], 0)
        return (accumulated, shifted), None

    (filtered, _), _ = lax.scan(apply_tap, (jnp.zeros((TOKENS, H), jnp.float32), product), jnp.arange(TAPS, dtype=jnp.int32))
    mixed_out = queries * (filtered + skip_bias[None, :] * product)
    return mixed_out.T.astype(jnp.bfloat16)
```

```python
import jax
import jax.numpy as jnp
from jax import lax
from jax.sharding import PartitionSpec as P


def toeplitz_rows(padded_taps):
    group_count, padded_len = padded_taps.shape
    tap_count = (padded_len - 1) // 2
    tiled = jnp.tile(padded_taps, (1, tap_count))
    trimmed = tiled[:, : tap_count * (padded_len - 1)]
    shaped = trimmed.reshape(group_count, tap_count, padded_len - 1)
    return shaped[:, :, tap_count : 2 * tap_count]


def long_convolution(product, long_filter):
    channel_count, seq_length = product.shape
    group_count, tap_count = long_filter.shape
    near_pad = jnp.concatenate(
        [
            jnp.zeros((group_count, tap_count), jnp.float32),
            long_filter,
            jnp.zeros((group_count, 1), jnp.float32),
        ],
        1,
    )
    far_pad = jnp.concatenate(
        [long_filter, jnp.zeros((group_count, tap_count + 1), jnp.float32)], 1
    )
    near_taps = toeplitz_rows(near_pad)
    far_taps = toeplitz_rows(far_pad)
    blocks = product.reshape(
        group_count, channel_count // group_count, seq_length // tap_count, tap_count
    )
    earlier = jnp.pad(blocks, ((0, 0), (0, 0), (1, 0), (0, 0)))[:, :, :-1]
    filtered = jnp.einsum("gcna,gab->gcnb", blocks, near_taps, precision=lax.Precision.HIGHEST)
    filtered = filtered + jnp.einsum(
        "gcna,gab->gcnb", earlier, far_taps, precision=lax.Precision.HIGHEST
    )
    return filtered.reshape(channel_count, seq_length)


def local(tokens, in_weight, short_weight, long_filter, skip_bias):
    mdl_count = lax.axis_size("mdl")
    local_chans, stream_count, feature_part = in_weight.shape
    channel_count = local_chans // mdl_count
    gathered = lax.all_gather(tokens, "tok", axis=0, tiled=True)
    seq_length = gathered.shape[0]
    weight_rows = in_weight.transpose(1, 0, 2).reshape(stream_count * local_chans, feature_part)
    partial = lax.dot_general(
        weight_rows, gathered, (((1,), (1,)), ((), ())), preferred_element_type=jnp.float32
    ).astype(jnp.bfloat16)
    partial = partial.reshape(stream_count, mdl_count, channel_count, seq_length)
    streams = lax.psum_scatter(partial, "mdl", scatter_dimension=1, tiled=True)
    streams = streams.reshape(stream_count, channel_count, seq_length).astype(jnp.float32)
    taps = short_weight.transpose(1, 2, 0)
    padded = jnp.pad(streams, ((0, 0), (0, 0), (2, 0)))
    featured = jnp.zeros_like(streams)
    for shift_index in range(3):
        featured = (
            featured
            + taps[:, shift_index, :, None]
            * padded[:, :, 2 - shift_index : 2 - shift_index + seq_length]
        )
    product = featured[1] * featured[2]
    filtered = long_convolution(product, long_filter)
    mixed_out = (featured[0] * (filtered + skip_bias[:, None] * product)).astype(jnp.bfloat16)
    return lax.all_to_all(mixed_out, "mdl", split_axis=1, concat_axis=0, tiled=True)


def solution(mesh):
    in_specs = (
        P(("grp", "tok"), "mdl"),
        P("tok", None, "mdl"),
        P(("tok", "mdl"), None, None),
        P(("tok", "mdl"), None),
        P(("tok", "mdl")),
    )
    out_specs = P("tok", ("grp", "mdl"))
    return jax.shard_map(local, mesh=mesh, in_specs=in_specs, out_specs=out_specs, check_vma=False)
```

```python
import jax
import jax.numpy as jnp
from jax import lax
from jax.experimental import pallas as pl
from jax.experimental.pallas import tpu as pltpu
from jax.sharding import PartitionSpec as P

MESH = pl.DeviceIdType.MESH
CHUNK = 128
SKEW = 2


def toeplitz_rows(padded_taps):
    group_count, padded_len = padded_taps.shape
    tap_count = (padded_len - 1) // 2
    tiled = jnp.tile(padded_taps, (1, tap_count))
    trimmed = tiled[:, : tap_count * (padded_len - 1)]
    shaped = trimmed.reshape(group_count, tap_count, padded_len - 1)
    return shaped[:, :, tap_count : 2 * tap_count]


def long_convolution(product, long_filter):
    channel_count, seq_length = product.shape
    group_count, tap_count = long_filter.shape
    near_pad = jnp.concatenate(
        [
            jnp.zeros((group_count, tap_count), jnp.float32),
            long_filter,
            jnp.zeros((group_count, 1), jnp.float32),
        ],
        1,
    )
    far_pad = jnp.concatenate(
        [long_filter, jnp.zeros((group_count, tap_count + 1), jnp.float32)], 1
    )
    near_taps = toeplitz_rows(near_pad)
    far_taps = toeplitz_rows(far_pad)
    blocks = product.reshape(
        group_count, channel_count // group_count, seq_length // tap_count, tap_count
    )
    earlier = jnp.pad(blocks, ((0, 0), (0, 0), (1, 0), (0, 0)))[:, :, :-1]
    filtered = jnp.einsum("gcna,gab->gcnb", blocks, near_taps, precision=lax.Precision.HIGHEST)
    filtered = filtered + jnp.einsum(
        "gcna,gab->gcnb", earlier, far_taps, precision=lax.Precision.HIGHEST
    )
    return filtered.reshape(channel_count, seq_length)


def local(tokens, in_weight, short_weight, long_filter, skip_bias):
    mdl_count = lax.axis_size("mdl")
    local_chans, stream_count, feature_part = in_weight.shape
    channel_count = local_chans // mdl_count
    gathered = lax.all_gather(tokens, "tok", axis=0, tiled=True)
    seq_length = gathered.shape[0]
    weight_rows = in_weight.transpose(1, 0, 2).reshape(stream_count * local_chans, feature_part)
    partial = lax.dot_general(
        weight_rows, gathered, (((1,), (1,)), ((), ())), preferred_element_type=jnp.float32
    ).astype(jnp.bfloat16)
    partial = partial.reshape(stream_count, mdl_count, channel_count, seq_length)
    streams = lax.psum_scatter(partial, "mdl", scatter_dimension=1, tiled=True)
    streams = streams.reshape(stream_count, channel_count, seq_length).astype(jnp.float32)
    taps = short_weight.transpose(1, 2, 0)
    padded = jnp.pad(streams, ((0, 0), (0, 0), (2, 0)))
    featured = jnp.zeros_like(streams)
    for shift_index in range(3):
        featured = (
            featured
            + taps[:, shift_index, :, None]
            * padded[:, :, 2 - shift_index : 2 - shift_index + seq_length]
        )
    product = featured[1] * featured[2]
    filtered = long_convolution(product, long_filter)
    mixed_out = (featured[0] * (filtered + skip_bias[:, None] * product)).astype(jnp.bfloat16)
    return lax.all_to_all(mixed_out, "mdl", split_axis=1, concat_axis=0, tiled=True)


def mixer_kernel(
    tokens_ref, weight_ref, param_ref, out_ref,
    weights, tok, inbox, outbox, summed, params, toeplitz, mixed,
    weight_sem, tok_load_sem, tok_send_sem, tok_recv_sem,
    param_load_sem, param_send_sem, param_recv_sem,
    send_sem, recv_sem, mixed_send_sem, mixed_recv_sem,
):
    z = lax.axis_index("mdl")
    me = lax.axis_index("tok")
    depth = lax.axis_size("mdl")
    rows, features = tokens_ref.shape
    streams, channels, _ = weight_ref.shape
    half = channels // 2
    chunks = half // CHUNK
    units = 4 * chunks
    own_channels = channels // depth
    taps = params.shape[-1]
    group = 16
    is_end = (z == 0) | (z == depth - 1)
    peer = me + 1 - 2 * (me % 2)
    across = me + 2 - 4 * (me // 2)
    far = 3 - me

    def block_rows(block):
        return pl.ds(pl.multiple_of(block * rows, rows), rows)

    def weight_copy(side, chunk):
        window = pl.ds(side * half + chunk * CHUNK, CHUNK)
        return pltpu.make_async_copy(
            weight_ref.at[:, window, :], weights.at[:, window, :], weight_sem.at[side, chunk]
        )

    def token_copy(index, source, block, target):
        return pltpu.make_async_remote_copy(
            source, tok.at[block_rows(block), :], tok_send_sem.at[index], tok_recv_sem.at[index],
            device_id={"tok": target}, device_id_type=MESH,
        )

    own_tokens = pltpu.make_async_copy(tokens_ref, tok.at[block_rows(me), :], tok_load_sem)
    own_tokens.start()
    own_params = pltpu.make_async_copy(param_ref, params.at[z % 2], param_load_sem)
    own_params.start()
    for chunk in range(chunks):
        for side in range(2):
            weight_copy(side, chunk).start()

    barrier = pltpu.get_barrier_semaphore()
    for step in range(1, depth):
        pl.semaphore_signal(barrier, inc=1, device_id={"mdl": (z + step) % depth}, device_id_type=MESH)
    for other in (peer, across):
        pl.semaphore_signal(barrier, inc=1, device_id={"tok": other}, device_id_type=MESH)
    pl.semaphore_wait(barrier, depth + 1)

    to_across = token_copy(1, tokens_ref, me, across)
    to_across.start()
    to_peer = token_copy(0, tokens_ref, me, peer)
    to_peer.start()
    forward = token_copy(2, tok.at[block_rows(across), :], across, peer)
    to_end = pltpu.make_async_remote_copy(
        param_ref, params.at[z % 2], param_send_sem, param_recv_sem,
        device_id={"mdl": (depth - 1) * (z // 2)}, device_id_type=MESH,
    )

    @pl.when(jnp.logical_not(is_end))
    def _():
        to_end.start()

    own_tokens.wait()
    own_params.wait()

    def unit_copy(side, unit):
        return pltpu.make_async_remote_copy(
            outbox.at[side, unit], inbox.at[side, unit],
            send_sem.at[side, unit], recv_sem.at[side, unit],
            device_id={"mdl": (z + 2 * side - 1 + depth) % depth}, device_id_type=MESH,
        )

    def mixed_copy(chunk, step):
        target = (z + step) % depth
        side = z // 2
        at_source = pl.ds(pl.multiple_of(chunk * CHUNK, CHUNK), CHUNK)
        at_target = pl.ds(pl.multiple_of(side * half + chunk * CHUNK, CHUNK), CHUNK)
        return pltpu.make_async_remote_copy(
            mixed.at[target, at_source, :], out_ref.at[at_target, :],
            mixed_send_sem.at[chunk, step - 1], mixed_recv_sem.at[side, chunk],
            device_id={"mdl": target}, device_id_type=MESH,
        )

    def place(unit):
        late = unit // (2 * chunks)
        rest = unit - 2 * chunks * late
        block = (1 - late) * (rest // chunks) + late * (2 + rest % 2)
        chunk = (1 - late) * (rest % chunks) + late * (rest // 2)
        return block, chunk

    def block_of(order):
        flipped_low = me % 2 + (order % 2) * (1 - 2 * (me % 2))
        flipped_high = me // 2 + (order // 2) * (1 - 2 * (me // 2))
        return 2 * flipped_high + flipped_low

    def work(side, step):
        position = z if side == 1 else depth - 1 - z
        unit = step - SKEW * position

        @pl.when((unit >= 0) & (unit < units))
        def _():
            order, chunk = place(unit)
            block = block_of(order)

            @pl.when(unit < chunks)
            def _():
                weight_copy(side, chunk).wait()

            window = pl.ds(pl.multiple_of(side * half + chunk * CHUNK, CHUNK), CHUNK)
            partial = lax.dot_general(
                weights[:, window, :].reshape(streams * CHUNK, features),
                tok[block_rows(block), :],
                (((1,), (1,)), ((), ())),
                preferred_element_type=jnp.float32,
            ).reshape(streams, CHUNK, rows)

            @pl.when(position == 0)
            def _():
                outbox[side, unit] = partial.astype(jnp.bfloat16)

            @pl.when(position > 0)
            def _():
                unit_copy(side, unit).wait_recv()
                total = partial + inbox[side, unit].astype(jnp.float32)

                @pl.when(position < depth - 1)
                def _():
                    outbox[side, unit] = total.astype(jnp.bfloat16)

                @pl.when(position == depth - 1)
                def _():
                    held = pl.ds(pl.multiple_of(chunk * CHUNK, CHUNK), CHUNK)
                    lanes = pl.ds(pl.multiple_of(block * rows, rows), rows)
                    summed[:, held, lanes] = total

            @pl.when(position < depth - 1)
            def _():
                @pl.when(unit >= 2)
                def _():
                    unit_copy(side, unit - 2).wait_send()

                unit_copy(side, unit).start()

    def make_toeplitz():
        def one(index, carry):
            slot = index // (own_channels // group)
            row = own_channels + index % (own_channels // group)
            line = jnp.concatenate(
                [params[slot, pl.ds(row, 1), :], jnp.zeros((1, taps), jnp.float32)], 1
            )
            wide = jnp.broadcast_to(line, (taps, 2 * taps))
            toeplitz[index] = pltpu.roll(wide, 0, 1, stride=1, stride_axis=0).astype(jnp.bfloat16)
            return carry

        lax.fori_loop(0, half // group, one, 0)

    def finish(chunk):
        def one(index, carry):
            channel = pl.multiple_of(chunk * CHUNK + index * group, group)
            slot = channel // own_channels
            row = pl.multiple_of(channel % own_channels, group)
            held = pl.ds(channel, group)
            scales = params[slot, pl.ds(row, group), :]
            length = summed.shape[-1]
            lane = lax.broadcasted_iota(jnp.int32, (group, length), 1)
            featured = []
            for stream in range(streams):
                value = summed[stream, held, :]
                feature = scales[:, 3 * stream : 3 * stream + 1] * value
                for shift in (1, 2):
                    moved = jnp.where(lane >= shift, pltpu.roll(value, shift, 1), 0.0)
                    at = 3 * stream + shift
                    feature = feature + scales[:, at : at + 1] * moved
                featured.append(feature)
            product = featured[1] * featured[2]
            blocks = length // taps
            stacked = jnp.concatenate(
                [product[:, n * taps : (n + 1) * taps] for n in range(blocks)], 0
            ).astype(jnp.bfloat16)
            spread = jnp.dot(
                stacked, toeplitz[channel // group], preferred_element_type=jnp.float32
            )
            for n in range(blocks):
                near = spread[n * group : (n + 1) * group, :taps]
                if n > 0:
                    near = near + spread[(n - 1) * group : n * group, taps:]
                cut = slice(n * taps, (n + 1) * taps)
                gated = featured[0][:, cut] * (near + scales[:, 9:10] * product[:, cut])
                mixed[n, held, :] = gated.astype(jnp.bfloat16)
            return carry

        lax.fori_loop(0, CHUNK // group, one, 0)
        at_source = pl.ds(pl.multiple_of(chunk * CHUNK, CHUNK), CHUNK)
        at_target = pl.ds(pl.multiple_of((z // 2) * half + chunk * CHUNK, CHUNK), CHUNK)
        for step in range(1, depth):
            mixed_copy(chunk, step).start()
        out_ref[at_target, :] = mixed[z, at_source, :]

    def timestep(step, carry):
        @pl.when(step == chunks)
        def _():
            to_peer.wait_recv()

        @pl.when(step == 2 * chunks - 1)
        def _():
            to_across.wait_recv()
            forward.start()

        @pl.when(step == 2 * chunks + 1)
        def _():
            forward.wait_recv()

        work(0, step)
        work(1, step)

        @pl.when(is_end & (step == 3))
        def _():
            pltpu.make_async_remote_copy(
                param_ref, params.at[(z + 1) % 2], param_send_sem, param_recv_sem,
                device_id={"mdl": (z + 1) % depth}, device_id_type=MESH,
            ).wait_recv()
            make_toeplitz()

        unit = step - SKEW * (depth - 1)

        @pl.when(is_end & (unit >= 2 * chunks) & (unit % 2 == 1))
        def _():
            finish((unit - 2 * chunks) // 2)

        return carry

    lax.fori_loop(0, units + SKEW * (depth - 1), timestep, 0)

    to_across.wait_send()
    to_peer.wait_send()
    forward.wait_send()

    @pl.when(jnp.logical_not(is_end))
    def _():
        to_end.wait_send()

    for side in range(2):
        position = z if side == 1 else depth - 1 - z

        @pl.when(position < depth - 1)
        def _():
            unit_copy(side, units - 2).wait_send()
            unit_copy(side, units - 1).wait_send()

        @pl.when(position < depth - 1)
        def _():
            for chunk in range(chunks):
                window = pl.ds(side * half + chunk * CHUNK, CHUNK)
                pltpu.make_async_remote_copy(
                    mixed.at[0, pl.ds(chunk * CHUNK, CHUNK), :], out_ref.at[window, :],
                    mixed_send_sem.at[chunk, 0], mixed_recv_sem.at[side, chunk],
                    device_id={"mdl": (z + 1) % depth}, device_id_type=MESH,
                ).wait_recv()

    @pl.when(is_end)
    def _():
        for chunk in range(chunks):
            for step in range(1, depth):
                mixed_copy(chunk, step).wait_send()


def local_fused(tokens, in_weight, short_weight, long_filter, skip_bias):
    depth = lax.axis_size("mdl")
    rows, features = tokens.shape
    channels, streams, _ = in_weight.shape
    groups, taps = long_filter.shape
    own_channels = channels // depth
    half = channels // 2
    chunks = half // CHUNK
    units = 4 * chunks
    length = rows * lax.axis_size("tok")
    scales = jnp.concatenate([short_weight.reshape(own_channels, streams * 3), skip_bias[:, None]], 1)
    scales = jnp.pad(scales, ((0, 0), (0, taps - scales.shape[1])))
    params = jnp.concatenate([scales, long_filter], 0)
    dma = pltpu.SemaphoreType.DMA
    return pl.pallas_call(
        mixer_kernel,
        out_shape=jax.ShapeDtypeStruct((channels, length // depth), jnp.bfloat16),
        in_specs=[pl.BlockSpec(memory_space=pl.ANY)] * 3,
        out_specs=pl.BlockSpec(memory_space=pltpu.VMEM),
        scratch_shapes=[
            pltpu.VMEM((streams, channels, features), jnp.bfloat16),
            pltpu.VMEM((length, features), jnp.bfloat16),
            pltpu.VMEM((2, units, streams, CHUNK, rows), jnp.bfloat16),
            pltpu.VMEM((2, units, streams, CHUNK, rows), jnp.bfloat16),
            pltpu.VMEM((streams, half, length), jnp.float32),
            pltpu.VMEM((2, own_channels + groups, taps), jnp.float32),
            pltpu.VMEM((half // 16, taps, 2 * taps), jnp.bfloat16),
            pltpu.VMEM((depth, half, length // depth), jnp.bfloat16),
            dma((2, chunks)),
            dma,
            dma((3,)),
            dma((3,)),
            dma,
            dma,
            dma,
            dma((2, units)),
            dma((2, units)),
            dma((chunks, depth - 1)),
            dma((2, chunks)),
        ],
        compiler_params=pltpu.CompilerParams(
            collective_id=0, has_side_effects=True, vmem_limit_bytes=52 * 1024 * 1024
        ),
        cost_estimate=pl.CostEstimate(
            flops=2 * length * streams * channels * features,
            bytes_accessed=2 * streams * channels * features,
            transcendentals=0,
        ),
    )(tokens, in_weight.transpose(1, 0, 2), params)


def solution(mesh):
    in_specs = (
        P(("grp", "tok"), "mdl"),
        P("tok", None, "mdl"),
        P(("tok", "mdl"), None, None),
        P(("tok", "mdl"), None),
        P(("tok", "mdl")),
    )
    out_specs = P("tok", ("grp", "mdl"))
    body = local_fused if mesh.shape["mdl"] == 4 and mesh.shape["tok"] == 4 else local
    return jax.shard_map(body, mesh=mesh, in_specs=in_specs, out_specs=out_specs, check_vma=False)
```

```python
import jax
import jax.numpy as jnp
from jax import lax
from jax.experimental import pallas as pl
from jax.experimental.pallas import tpu as pltpu
from jax.sharding import PartitionSpec as P

MESH = pl.DeviceIdType.MESH
CHUNK = 128
SKEW = 2
AHEAD = 8


def toeplitz_rows(padded_taps):
    group_count, padded_len = padded_taps.shape
    tap_count = (padded_len - 1) // 2
    tiled = jnp.tile(padded_taps, (1, tap_count))
    trimmed = tiled[:, : tap_count * (padded_len - 1)]
    shaped = trimmed.reshape(group_count, tap_count, padded_len - 1)
    return shaped[:, :, tap_count : 2 * tap_count]


def long_convolution(product, long_filter):
    channel_count, seq_length = product.shape
    group_count, tap_count = long_filter.shape
    near_pad = jnp.concatenate(
        [
            jnp.zeros((group_count, tap_count), jnp.float32),
            long_filter,
            jnp.zeros((group_count, 1), jnp.float32),
        ],
        1,
    )
    far_pad = jnp.concatenate(
        [long_filter, jnp.zeros((group_count, tap_count + 1), jnp.float32)], 1
    )
    near_taps = toeplitz_rows(near_pad)
    far_taps = toeplitz_rows(far_pad)
    blocks = product.reshape(
        group_count, channel_count // group_count, seq_length // tap_count, tap_count
    )
    earlier = jnp.pad(blocks, ((0, 0), (0, 0), (1, 0), (0, 0)))[:, :, :-1]
    filtered = jnp.einsum("gcna,gab->gcnb", blocks, near_taps, precision=lax.Precision.HIGHEST)
    filtered = filtered + jnp.einsum(
        "gcna,gab->gcnb", earlier, far_taps, precision=lax.Precision.HIGHEST
    )
    return filtered.reshape(channel_count, seq_length)


def local(tokens, in_weight, short_weight, long_filter, skip_bias):
    mdl_count = lax.axis_size("mdl")
    local_chans, stream_count, feature_part = in_weight.shape
    channel_count = local_chans // mdl_count
    gathered = lax.all_gather(tokens, "tok", axis=0, tiled=True)
    seq_length = gathered.shape[0]
    weight_rows = in_weight.transpose(1, 0, 2).reshape(stream_count * local_chans, feature_part)
    partial = lax.dot_general(
        weight_rows, gathered, (((1,), (1,)), ((), ())), preferred_element_type=jnp.float32
    ).astype(jnp.bfloat16)
    partial = partial.reshape(stream_count, mdl_count, channel_count, seq_length)
    streams = lax.psum_scatter(partial, "mdl", scatter_dimension=1, tiled=True)
    streams = streams.reshape(stream_count, channel_count, seq_length).astype(jnp.float32)
    taps = short_weight.transpose(1, 2, 0)
    padded = jnp.pad(streams, ((0, 0), (0, 0), (2, 0)))
    featured = jnp.zeros_like(streams)
    for shift_index in range(3):
        featured = (
            featured
            + taps[:, shift_index, :, None]
            * padded[:, :, 2 - shift_index : 2 - shift_index + seq_length]
        )
    product = featured[1] * featured[2]
    filtered = long_convolution(product, long_filter)
    mixed_out = (featured[0] * (filtered + skip_bias[:, None] * product)).astype(jnp.bfloat16)
    return lax.all_to_all(mixed_out, "mdl", split_axis=1, concat_axis=0, tiled=True)


def mixer_kernel(
    tokens_ref, weight_ref, param_ref, out_ref,
    weights, tok, inbox, outbox, summed, params, toeplitz, mixed,
    weight_sem, tok_load_sem, tok_send_sem, tok_recv_sem,
    param_load_sem, param_send_sem, param_recv_sem,
    send_sem, recv_sem, mixed_send_sem, mixed_recv_sem,
):
    z = lax.axis_index("mdl")
    me = lax.axis_index("tok")
    depth = lax.axis_size("mdl")
    rows, features = tokens_ref.shape
    streams, channels, _ = weight_ref.shape
    half = channels // 2
    chunks = half // CHUNK
    units = 4 * chunks
    own_channels = channels // depth
    taps = params.shape[-1]
    group = 16
    is_end = (z == 0) | (z == depth - 1)
    peer = me + 1 - 2 * (me % 2)
    across = me + 2 - 4 * (me // 2)
    far = 3 - me

    def block_rows(block):
        return pl.ds(pl.multiple_of(block * rows, rows), rows)

    def weight_copy(side, chunk):
        window = pl.ds(side * half + chunk * CHUNK, CHUNK)
        return pltpu.make_async_copy(
            weight_ref.at[:, window, :], weights.at[:, window, :], weight_sem.at[side, chunk]
        )

    def token_copy(index, source, block, target):
        return pltpu.make_async_remote_copy(
            source, tok.at[block_rows(block), :], tok_send_sem.at[index], tok_recv_sem.at[index],
            device_id={"tok": target}, device_id_type=MESH,
        )

    own_tokens = pltpu.make_async_copy(tokens_ref, tok.at[block_rows(me), :], tok_load_sem)
    own_tokens.start()
    own_params = pltpu.make_async_copy(param_ref, params.at[z % 2], param_load_sem)
    own_params.start()
    for chunk in range(chunks):
        for side in range(2):
            weight_copy(side, chunk).start()

    barrier = pltpu.get_barrier_semaphore()
    for step in range(1, depth):
        pl.semaphore_signal(barrier, inc=1, device_id={"mdl": (z + step) % depth}, device_id_type=MESH)
    for other in (peer, across):
        pl.semaphore_signal(barrier, inc=1, device_id={"tok": other}, device_id_type=MESH)
    pl.semaphore_wait(barrier, depth + 1)

    to_across = token_copy(1, tokens_ref, me, across)
    to_across.start()
    to_peer = token_copy(0, tokens_ref, me, peer)
    to_peer.start()
    forward = token_copy(2, tok.at[block_rows(across), :], across, peer)
    to_end = pltpu.make_async_remote_copy(
        param_ref, params.at[z % 2], param_send_sem, param_recv_sem,
        device_id={"mdl": (depth - 1) * (z // 2)}, device_id_type=MESH,
    )

    @pl.when(jnp.logical_not(is_end))
    def _():
        to_end.start()

    own_tokens.wait()
    own_params.wait()

    def unit_copy(side, unit):
        return pltpu.make_async_remote_copy(
            outbox.at[side, unit], inbox.at[side, unit],
            send_sem.at[side, unit], recv_sem.at[side, unit],
            device_id={"mdl": (z + 2 * side - 1 + depth) % depth}, device_id_type=MESH,
        )

    def mixed_copy(chunk, step):
        target = (z + step) % depth
        side = z // 2
        at_source = pl.ds(pl.multiple_of(chunk * CHUNK, CHUNK), CHUNK)
        at_target = pl.ds(pl.multiple_of(side * half + chunk * CHUNK, CHUNK), CHUNK)
        return pltpu.make_async_remote_copy(
            mixed.at[target, at_source, :], out_ref.at[at_target, :],
            mixed_send_sem.at[chunk, step - 1], mixed_recv_sem.at[side, chunk],
            device_id={"mdl": target}, device_id_type=MESH,
        )

    def place(unit):
        late = unit // (2 * chunks)
        rest = unit - 2 * chunks * late
        block = (1 - late) * (rest // chunks) + late * (2 + rest % 2)
        chunk = (1 - late) * (rest % chunks) + late * (rest // 2)
        return block, chunk

    def block_of(order):
        flipped_low = me % 2 + (order % 2) * (1 - 2 * (me % 2))
        flipped_high = me // 2 + (order // 2) * (1 - 2 * (me // 2))
        return 2 * flipped_high + flipped_low

    def work(side, step):
        position = z if side == 1 else depth - 1 - z
        unit = step - SKEW * position

        @pl.when((unit >= 0) & (unit < units))
        def _():
            order, chunk = place(unit)
            block = block_of(order)

            @pl.when(unit < chunks)
            def _():
                weight_copy(side, chunk).wait()

            window = pl.ds(pl.multiple_of(side * half + chunk * CHUNK, CHUNK), CHUNK)
            partial = lax.dot_general(
                weights[:, window, :].reshape(streams * CHUNK, features),
                tok[block_rows(block), :],
                (((1,), (1,)), ((), ())),
                preferred_element_type=jnp.float32,
            ).reshape(streams, CHUNK, rows)

            @pl.when(position == 0)
            def _():
                outbox[side, unit] = partial.astype(jnp.bfloat16)

            @pl.when(position > 0)
            def _():
                unit_copy(side, unit).wait_recv()
                total = partial + inbox[side, unit].astype(jnp.float32)

                @pl.when(position < depth - 1)
                def _():
                    outbox[side, unit] = total.astype(jnp.bfloat16)

                @pl.when(position == depth - 1)
                def _():
                    held = pl.ds(pl.multiple_of(chunk * CHUNK, CHUNK), CHUNK)
                    lanes = pl.ds(pl.multiple_of(block * rows, rows), rows)
                    summed[:, held, lanes] = total

            @pl.when(position < depth - 1)
            def _():
                @pl.when(unit >= AHEAD)
                def _():
                    unit_copy(side, unit - AHEAD).wait_send()

                unit_copy(side, unit).start()

    def make_toeplitz():
        def one(index, carry):
            slot = index // (own_channels // group)
            row = own_channels + index % (own_channels // group)
            line = jnp.concatenate(
                [params[slot, pl.ds(row, 1), :], jnp.zeros((1, taps), jnp.float32)], 1
            )
            wide = jnp.broadcast_to(line, (taps, 2 * taps))
            toeplitz[index] = pltpu.roll(wide, 0, 1, stride=1, stride_axis=0).astype(jnp.bfloat16)
            return carry

        lax.fori_loop(0, half // group, one, 0)

    def finish(chunk):
        def one(index, carry):
            channel = pl.multiple_of(chunk * CHUNK + index * group, group)
            slot = channel // own_channels
            row = pl.multiple_of(channel % own_channels, group)
            held = pl.ds(channel, group)
            scales = params[slot, pl.ds(row, group), :]
            length = summed.shape[-1]
            lane = lax.broadcasted_iota(jnp.int32, (group, length), 1)
            featured = []
            for stream in range(streams):
                value = summed[stream, held, :]
                feature = scales[:, 3 * stream : 3 * stream + 1] * value
                for shift in (1, 2):
                    moved = jnp.where(lane >= shift, pltpu.roll(value, shift, 1), 0.0)
                    at = 3 * stream + shift
                    feature = feature + scales[:, at : at + 1] * moved
                featured.append(feature)
            product = featured[1] * featured[2]
            blocks = length // taps
            stacked = jnp.concatenate(
                [product[:, n * taps : (n + 1) * taps] for n in range(blocks)], 0
            ).astype(jnp.bfloat16)
            spread = jnp.dot(
                stacked, toeplitz[channel // group], preferred_element_type=jnp.float32
            )
            for n in range(blocks):
                near = spread[n * group : (n + 1) * group, :taps]
                if n > 0:
                    near = near + spread[(n - 1) * group : n * group, taps:]
                cut = slice(n * taps, (n + 1) * taps)
                gated = featured[0][:, cut] * (near + scales[:, 9:10] * product[:, cut])
                mixed[n, held, :] = gated.astype(jnp.bfloat16)
            return carry

        lax.fori_loop(0, CHUNK // group, one, 0)
        at_source = pl.ds(pl.multiple_of(chunk * CHUNK, CHUNK), CHUNK)
        at_target = pl.ds(pl.multiple_of((z // 2) * half + chunk * CHUNK, CHUNK), CHUNK)
        for step in range(1, depth):
            mixed_copy(chunk, step).start()
        out_ref[at_target, :] = mixed[z, at_source, :]

    def timestep(step, carry):
        @pl.when(step == chunks)
        def _():
            to_peer.wait_recv()

        @pl.when(step == 2 * chunks - 1)
        def _():
            to_across.wait_recv()
            forward.start()

        @pl.when(step == 2 * chunks + 1)
        def _():
            forward.wait_recv()

        work(0, step)
        work(1, step)

        @pl.when(is_end & (step == 3))
        def _():
            pltpu.make_async_remote_copy(
                param_ref, params.at[(z + 1) % 2], param_send_sem, param_recv_sem,
                device_id={"mdl": (z + 1) % depth}, device_id_type=MESH,
            ).wait_recv()
            make_toeplitz()

        unit = step - SKEW * (depth - 1)

        @pl.when(is_end & (unit >= 2 * chunks) & (unit % 2 == 1))
        def _():
            finish((unit - 2 * chunks) // 2)

        return carry

    lax.fori_loop(0, units + SKEW * (depth - 1), timestep, 0)

    to_across.wait_send()
    to_peer.wait_send()
    forward.wait_send()

    @pl.when(jnp.logical_not(is_end))
    def _():
        to_end.wait_send()

    for side in range(2):
        position = z if side == 1 else depth - 1 - z

        @pl.when(position < depth - 1)
        def _():
            for last in range(AHEAD):
                unit_copy(side, units - AHEAD + last).wait_send()

        @pl.when(position < depth - 1)
        def _():
            for chunk in range(chunks):
                window = pl.ds(side * half + chunk * CHUNK, CHUNK)
                pltpu.make_async_remote_copy(
                    mixed.at[0, pl.ds(chunk * CHUNK, CHUNK), :], out_ref.at[window, :],
                    mixed_send_sem.at[chunk, 0], mixed_recv_sem.at[side, chunk],
                    device_id={"mdl": (z + 1) % depth}, device_id_type=MESH,
                ).wait_recv()

    @pl.when(is_end)
    def _():
        for chunk in range(chunks):
            for step in range(1, depth):
                mixed_copy(chunk, step).wait_send()


def local_fused(tokens, in_weight, short_weight, long_filter, skip_bias):
    depth = lax.axis_size("mdl")
    rows, features = tokens.shape
    channels, streams, _ = in_weight.shape
    groups, taps = long_filter.shape
    own_channels = channels // depth
    half = channels // 2
    chunks = half // CHUNK
    units = 4 * chunks
    length = rows * lax.axis_size("tok")
    scales = jnp.concatenate([short_weight.reshape(own_channels, streams * 3), skip_bias[:, None]], 1)
    scales = jnp.pad(scales, ((0, 0), (0, taps - scales.shape[1])))
    params = jnp.concatenate([scales, long_filter], 0)
    dma = pltpu.SemaphoreType.DMA
    return pl.pallas_call(
        mixer_kernel,
        out_shape=jax.ShapeDtypeStruct((channels, length // depth), jnp.bfloat16),
        in_specs=[pl.BlockSpec(memory_space=pl.ANY)] * 3,
        out_specs=pl.BlockSpec(memory_space=pltpu.VMEM),
        scratch_shapes=[
            pltpu.VMEM((streams, channels, features), jnp.bfloat16),
            pltpu.VMEM((length, features), jnp.bfloat16),
            pltpu.VMEM((2, units, streams, CHUNK, rows), jnp.bfloat16),
            pltpu.VMEM((2, units, streams, CHUNK, rows), jnp.bfloat16),
            pltpu.VMEM((streams, half, length), jnp.float32),
            pltpu.VMEM((2, own_channels + groups, taps), jnp.float32),
            pltpu.VMEM((half // 16, taps, 2 * taps), jnp.bfloat16),
            pltpu.VMEM((depth, half, length // depth), jnp.bfloat16),
            dma((2, chunks)),
            dma,
            dma((3,)),
            dma((3,)),
            dma,
            dma,
            dma,
            dma((2, units)),
            dma((2, units)),
            dma((chunks, depth - 1)),
            dma((2, chunks)),
        ],
        compiler_params=pltpu.CompilerParams(
            collective_id=0, has_side_effects=True, vmem_limit_bytes=52 * 1024 * 1024
        ),
        cost_estimate=pl.CostEstimate(
            flops=2 * length * streams * channels * features,
            bytes_accessed=2 * streams * channels * features,
            transcendentals=0,
        ),
    )(tokens, in_weight.transpose(1, 0, 2), params)


def solution(mesh):
    in_specs = (
        P(("grp", "tok"), "mdl"),
        P("tok", None, "mdl"),
        P(("tok", "mdl"), None, None),
        P(("tok", "mdl"), None),
        P(("tok", "mdl")),
    )
    out_specs = P("tok", ("grp", "mdl"))
    body = local_fused if mesh.shape["mdl"] == 4 and mesh.shape["tok"] == 4 else local
    return jax.shard_map(body, mesh=mesh, in_specs=in_specs, out_specs=out_specs, check_vma=False)
```
